32 devices in a mesh: section: 2 (over x), dp: 4 (over z), mp: 4 (over y, core).
Axes of the slice: x: 2, y: 2, z: 4, core: 2. Of those that a mesh axis runs over, the one named last changes fastest.
Arguments:
- activations: bfloat16 [2, 64, 12288], P('section', 'dp', 'mp'), may hold values from -50 to 50, as said below
- norm_gain: bfloat16 [2, 12288], P('section', 'mp'), may hold values from 0.25 to 1.75
- norm_shift: bfloat16 [2, 12288], P('section', 'mp'), may hold values from -3 to 3
- up_weight: bfloat16 [2, 12288, 49152], P('section', 'mp', 'dp'), may hold values from -0.0546875 to 0.0546875
- up_bias: bfloat16 [2, 49152], P('section', 'dp'), may hold values from -3 to 3
Outputs:
- hidden: bfloat16 [2, 64, 49152], P('section', 'mp', 'dp')
The draws below stay inside these ranges and needn't reach their ends.
Inputs may be any that keep to these rules, and one draw needn't show every extreme that they name: Real-valued activations.
All inputs are finite; a program needn't handle non-finite values.
Results may differ from the reference program's by a relative error of at most 0.014.
Values may be sent and summed in bfloat16 or wider, within the bound.
No kernel may reach another device: no remote copies, remote signals or barrier semaphores. Data moves between devices by JAX's collectives and lax.ppermute only.
A program may use at most 128 MiB of HBM per device.

```python
import jax
import jax.numpy as jnp
from jax import lax

D = 12288
FF = 49152
TOKENS = 64
N_MP = 4


def draw_activations(key, part):
    keys = jax.random.split(jax.random.fold_in(key, 7), 4)
    position = jnp.arange(D, dtype=jnp.float32) / D
    column_scale = 0.6 * jnp.exp(jnp.log(3.0) * position) * jax.random.uniform(keys[0], (D,), jnp.float32, 0.5, 1.5)
    row_offset = jax.random.uniform(keys[1], (2, TOKENS, 1), jnp.float32, -1.0, 1.0)
    column_offset = jax.random.uniform(keys[2], (D,), jnp.float32, 0.0, 1.0)
    noise = jnp.clip(jax.random.normal(keys[3], (2, TOKENS, D), jnp.float32), -4.0, 4.0)
    row_scale = jnp.ones((2, TOKENS, 1), jnp.float32)
    values = row_offset + column_offset + row_scale * column_scale * noise
    return values.astype(jnp.bfloat16)


def block_levels(rng, extent, cuts, low, high):
    level = 1.0
    for dim, blocks in cuts:
        heights = jax.random.uniform(jax.random.fold_in(jax.random.fold_in(rng, 6), dim), (blocks,), jnp.float32, low / len(cuts), high / len(cuts))
        level = level * jnp.repeat(jnp.exp(heights), extent[dim] // blocks).reshape((-1,) + (1,) * (len(extent) - 1 - dim))
    return level


def centred(rng, shape, width, most, cuts=(), kind=jnp.bfloat16):
    result = jax.random.normal(rng, shape, jnp.float32) * width
    if len(cuts) > 0:
        result = block_levels(rng, shape, cuts, -0.22, 0.18) * result
    return jnp.clip(result, min=-most, max=most).astype(kind)


def setup_inputs(seed: int = 0) -> dict:
    streams_of = jax.random.split(jax.random.key(seed), 6)
    activations = draw_activations(jax.random.fold_in(streams_of[5], 71), 0)
    norm_gain = jnp.clip(1.0 + 0.15 * jax.random.normal(streams_of[1], (2, D), jnp.float32), 0.25, 1.75).astype(jnp.bfloat16)
    norm_shift = centred(streams_of[2], (2, D), 0.5, 3.0, ((0, 2), (1, 4)))
    up_weight = centred(streams_of[3], (2, D, FF), D ** -0.5, 0.0546875, ((0, 2), (1, 4), (2, 4)))
    up_bias = centred(streams_of[4], (2, FF), 0.5, 3.0, ((0, 2), (1, 4)))
    return dict(activations=activations, norm_gain=norm_gain, norm_shift=norm_shift, up_weight=up_weight, up_bias=up_bias)


def section_layer(source, gain, shift, weight, bias):
    values = source.astype(jnp.float32)
    average = lax.optimization_barrier(jnp.mean(values, axis=1, keepdims=True))
    moment = lax.optimization_barrier(jnp.mean(values * values, axis=1, keepdims=True))
    scaled = (values - average) * lax.rsqrt(moment - average * average + 1e-05)
    normed = (scaled * gain.astype(jnp.float32) + shift.astype(jnp.float32)).astype(jnp.bfloat16)
    block_width = D // N_MP
    total = jnp.zeros((TOKENS, FF), jnp.float32)
    for block in range(N_MP):
        lower = block * block_width
        partial_term = jnp.dot(normed[:, lower:lower + block_width], weight[lower:lower + block_width, :], preferred_element_type=jnp.float32)
        rounded = lax.optimization_barrier(partial_term.astype(jnp.bfloat16))
        total = total + rounded.astype(jnp.float32)
    total = total + bias.astype(jnp.float32)
    return jax.nn.gelu(total, approximate=True).astype(jnp.bfloat16)

def reference(activations, norm_gain, norm_shift, up_weight, up_bias):
    first = section_layer(activations[1], norm_gain[0], norm_shift[0], up_weight[0], up_bias[0])
    second = section_layer(activations[0], norm_gain[1], norm_shift[1], up_weight[1], up_bias[1])
    return jnp.stack([first, second])
```

```python
import functools

import jax
import jax.numpy as jnp
from jax import lax
from jax.experimental import pallas as pl
from jax.experimental.pallas import tpu as pltpu
from jax.sharding import PartitionSpec as P

EPS = 1e-05
LANES = 128
MIB = 1 << 20
VM = pl.BlockSpec(memory_space=pltpu.VMEM)
HB = pl.BlockSpec(memory_space=pl.ANY)
KEPT = 16
PARTS = 4
TILES = 24
SLOTS = 12
FIRST = 7
STEPS = ((0, 8), (6, 12), (12, 18), (16, 21), (21, 24), (24, 24))


def plan(columns):
    if columns % (TILES * LANES) == 0 and columns >= TILES * 512:
        return columns // TILES, SLOTS, FIRST, STEPS
    tile = next(u for u in (256, 128, columns) if columns % u == 0)
    tiles = columns // tile
    return tile, tiles, tiles, ((0, tiles), (tiles - tiles // 2, tiles), (tiles, tiles))


def params(rows):
    return pltpu.CompilerParams(vmem_limit_bytes=(24 if rows > 256 else 8) * MIB)


def cost(flops, read):
    return pl.CostEstimate(flops=int(flops), bytes_accessed=int(read), transcendentals=0)


def fetches(weight, ring, sem, tile, slots, low, high):
    copies = []
    depth = weight.shape[1]
    step = depth // PARTS
    while low < high:
        slot = low % slots
        count = min(high - low, slots - slot)
        for i in range(PARTS):
            rows = pl.ds(i * step, step)
            copies.append(
                pltpu.make_async_copy(
                    weight.at[0, rows, pl.ds(low * tile, count * tile)],
                    ring.at[rows, pl.ds(slot * tile, count * tile)],
                    sem.at[len(copies)],
                )
            )
        low += count
    return copies


def fetch_kernel(tile, slots, first, weight, ring, sem):
    copies = fetches(weight, ring, sem, tile, slots, 0, first)
    for copy in copies:
        copy.start()
    for copy in copies:
        copy.wait()


def fetch(weight, tile, slots, first, rows):
    depth = weight.shape[1]
    return pl.pallas_call(
        functools.partial(fetch_kernel, tile, slots, first),
        out_shape=pltpu.VMEM((depth, slots * tile), weight.dtype),
        in_specs=[HB],
        out_specs=VM,
        scratch_shapes=[pltpu.SemaphoreType.DMA((2 * PARTS,))],
        compiler_params=params(rows),
        cost_estimate=cost(0, depth * first * tile * 2),
        name="fetch",
    )(weight)


def prepare(places, gain, shift, pieces, x_ref, stat_ref):
    rows, width = pieces[0].shape
    tokens = rows * len(pieces)
    gains = gain[...].astype(jnp.float32)
    shifts = shift[...].astype(jnp.float32)
    first = lax.broadcasted_iota(jnp.int32, (16, LANES), 1) < LANES // 2
    for k, piece in enumerate(pieces):
        for sub in range(rows // 16):
            values = piece[pl.ds(sub * 16, 16), :].astype(jnp.float32)
            average = jnp.sum(values, axis=1, keepdims=True) / width
            centred = values - average
            spread = jnp.sum(centred * centred, axis=1, keepdims=True)
            place = pl.ds(pl.multiple_of(places[k] + sub * 16, 16), 16)
            x_ref[place, :] = (centred * gains).astype(jnp.bfloat16)
            stat_ref[place, :] = jnp.where(first, average, spread)
    row = lax.broadcasted_iota(jnp.int32, (16, width), 0)
    extra = jnp.where(row == 0, gains, jnp.where(row == 1, shifts, 0.0))
    x_ref[pl.ds(tokens, 16), :] = extra.astype(jnp.bfloat16)
    rest = x_ref.shape[0] - tokens - 16
    x_ref[pl.ds(tokens + 16, rest), :] = jnp.zeros((rest, width), jnp.bfloat16)


def product(x_ref, ring, tile, slots, index):
    at = pl.ds(pl.multiple_of(lax.rem(index, slots) * tile, tile), tile)
    return jnp.dot(x_ref[...], ring[:, at], preferred_element_type=jnp.float32)


def open_kernel(config, *refs):
    count, direct, tile, slots, low, high, blocks, total = config
    gain, shift = refs[:2]
    pieces = refs[2 : 2 + count]
    _, weight, ring, x_ref, stat_ref, sem = refs[2 + count :]
    copies = fetches(weight, ring, sem, tile, slots, low, high)
    for copy in copies:
        copy.start()

    mine = lax.axis_index("mp")
    size = pieces[0].shape[0]
    block = total // blocks
    owners = list(range(blocks))
    if direct:
        me = lax.axis_index("dp")
        owners = [lax.rem(me + count - k, count) for k in range(count)]
    places = [((o * size // block) ^ mine) * block + (o * size) % block for o in owners]

    @pl.when(mine >= 0)
    def _():
        prepare(places, gain, shift, pieces, x_ref, stat_ref)

    for copy in copies:
        copy.wait()


def raw_kernel(config, x_ref, _, weight, ring, acc_ref, sem):
    tile, slots, low, high = config
    copies = fetches(weight, ring, sem, tile, slots, low, high)
    for copy in copies:
        copy.start()
    rows, width = acc_ref.shape

    @pl.loop(0, width // tile)
    def _(i):
        acc = product(x_ref, ring, tile, slots, i)
        acc_ref[:, pl.ds(pl.multiple_of(i * tile, tile), tile)] = acc[:rows]

    for copy in copies:
        copy.wait()


def merge_kernel(tile, keep, got, *refs):
    kept, away = refs[-2:]
    block = got.shape[0] // 2

    @pl.loop(0, got.shape[1] // tile)
    def _(i):
        at = pl.ds(pl.multiple_of(i * tile, tile), tile)
        total = keep[:, at] + got[:, at].astype(jnp.float32)
        kept[:, at] = total[:block]
        away[:, at] = total[block:].astype(away.dtype)


def merge(keep, got, ring, tile, rows):
    height, width = got.shape[0] // 2, got.shape[1]
    through = [] if ring is None else [ring]
    outs = [pltpu.VMEM(ring.shape, ring.dtype)] if through else []
    outs.append(pltpu.VMEM((height, width), jnp.float32))
    outs.append(pltpu.VMEM((height, width), jnp.bfloat16))
    result = pl.pallas_call(
        functools.partial(merge_kernel, tile),
        out_shape=tuple(outs),
        in_specs=[VM] * (2 + len(through)),
        out_specs=(VM,) * len(outs),
        input_output_aliases={2: 0} if through else {},
        compiler_params=params(rows),
        name="merge",
    )(keep, got, *through)
    return result if through else (None,) + tuple(result)


def coefficients(stats, depth):
    count = len(stats)
    block = stats[0].shape[0] // count

    def parts(lane):
        columns = []
        for j, stat in enumerate(stats):
            whole = stat[:, lane : lane + 1]
            rows = [whole[(b ^ j) * block : ((b ^ j) + 1) * block] for b in range(count)]
            columns.append(jnp.concatenate(rows, axis=0))
        return columns

    averages = parts(0)
    average = sum(averages) / count
    spread = sum(parts(LANES // 2))
    for one in averages:
        spread = spread + depth * (one - average) * (one - average)
    scale = lax.rsqrt(spread / (depth * count) + EPS)
    return scale, averages[0] - average


def activate(bias, low, kept, got, out, start, tile):
    @pl.loop(0, kept.shape[1] // tile)
    def _(i):
        at = pl.multiple_of(i * tile, tile)
        total = kept[:, pl.ds(at, tile)] + got[:, pl.ds(at, tile)].astype(jnp.float32)
        total = total + bias[:, pl.ds(pl.multiple_of(low + at, tile), tile)].astype(jnp.float32)
        result = jax.nn.gelu(total, approximate=True).astype(out.dtype)
        out[:, pl.ds(pl.multiple_of(start + at, tile), tile)] = result


def layer_kernel(config, *refs):
    blocks, depth, tile, slots, base, done, low, high, later, ended, tokens = config
    refs = list(refs)
    take = lambda n: [refs.pop(0) for _ in range(n)]
    x_ref, ring = take(2)
    weight = take(1)[0]
    stats = take(blocks)
    earlier = take(1)[0] if later else None
    bias, kept, got = take(3) if ended is not None else (None,) * 3
    ring = take(1)[0]
    send, keep = take(2)
    out = take(1)[0] if ended is not None else None
    copies = fetches(weight, ring, refs[0], tile, slots, low, high)
    for copy in copies:
        copy.start()
    block = tokens // blocks
    scale, offset = coefficients([s[...] for s in stats], depth)

    def emit(acc, at):
        gains = acc[tokens : tokens + 1]
        shifts = acc[tokens + 1 : tokens + 2]
        values = scale * (acc[:tokens] + offset * gains) + shifts
        for j in range(blocks):
            part = values[j * block : (j + 1) * block]
            place = send if j % 2 else keep
            place[pl.ds((j // 2) * block, block), at] = part.astype(place.dtype)

    start = 0
    if later:
        start = earlier.shape[1]

        @pl.loop(0, start // tile)
        def _(i):
            at = pl.ds(pl.multiple_of(i * tile, tile), tile)
            emit(earlier[:, at], at)

    @pl.loop(0, done - base)
    def _(i):
        acc = product(x_ref, ring, tile, slots, base + i)
        emit(acc, pl.ds(pl.multiple_of(start + i * tile, tile), tile))

    if ended is not None:
        activate(bias, ended, kept, got, out, 0, tile)
    for copy in copies:
        copy.wait()


def layer(x, ring, weight, tile, slots, base, step, stats, earlier, ended, blocks, tokens, low):
    rows = x.shape[0]
    depth = weight.shape[1]
    done, high = step
    args = [x, ring, weight]
    outs = [pltpu.VMEM(ring.shape, ring.dtype)]
    specs = [VM, VM, HB]
    more = list(stats) + ([] if earlier is None else [earlier])
    if ended is not None:
        more += list(ended[1:])
    args += more
    specs += [VM] * len(more)
    width = (done - base) * tile + (0 if earlier is None else earlier.shape[1])
    outs.append(pltpu.VMEM((tokens // 2, width), jnp.bfloat16))
    outs.append(pltpu.VMEM((tokens // 2, width), jnp.float32))
    if ended is not None:
        outs.append(pltpu.VMEM(ended[2].shape, jnp.bfloat16))
    config = (
        blocks,
        depth,
        tile,
        slots,
        base,
        done,
        low,
        high,
        earlier is not None,
        None if ended is None else ended[0],
        tokens,
    )
    read = depth * max(high - low, (done - base) / 2) * tile * 2
    got = list(
        pl.pallas_call(
            functools.partial(layer_kernel, config),
            out_shape=tuple(outs),
            in_specs=specs,
            out_specs=(VM,) * len(outs),
            scratch_shapes=[pltpu.SemaphoreType.DMA((2 * PARTS,))],
            input_output_aliases={1: 0},
            compiler_params=params(rows),
            cost_estimate=cost(2 * rows * depth * (done - base) * tile, read),
            name="layer",
        )(*args)
    )
    return got.pop(0), got


def finale_kernel(config, *refs):
    edges, ready, tile = config
    out = refs[-1].at[0]
    bias = refs[0]
    if ready:
        start, part = refs[1], refs[1]
        width = part.shape[1]
        out[:, pl.ds(0, width)] = part[...]
        refs = refs[1:]
    for g, low in enumerate(edges):
        kept, got = refs[1 + 2 * g], refs[2 + 2 * g]
        activate(bias, low, kept, got, out, low, tile)


def finale(bias, ready, edges, groups, tile, rows):
    args = [bias] + ([] if ready is None else [ready])
    for kept, got in groups:
        args += [kept, got]
    height = groups[0][0].shape[0]
    return pl.pallas_call(
        functools.partial(finale_kernel, (tuple(edges), ready is not None, tile)),
        out_shape=jax.ShapeDtypeStruct((1, height, bias.shape[1]), jnp.bfloat16),
        in_specs=[VM] * len(args),
        out_specs=VM,
        compiler_params=params(rows),
        name="finale",
    )(*args)


def exchange(value, axis, by):
    size = lax.axis_size(axis)
    return lax.ppermute(value, axis, [(i, i ^ by) for i in range(size)])


def gather(block):
    sections, places = lax.axis_size("section"), lax.axis_size("dp")
    if places > 8:
        received = lax.ppermute(
            block, "section", [(s, (s + 1) % sections) for s in range(sections)]
        )
        return [lax.all_gather(received, "dp", axis=0, tiled=True)]
    pieces = []
    for k in range(places):
        pairs = [
            (s * places + d, ((s + 1) % sections) * places + (d + k) % places)
            for s in range(sections)
            for d in range(places)
        ]
        pieces.append(lax.ppermute(block, ("section", "dp"), pairs))
    return pieces


def halved(send, keep, blocks, block):
    by, left = 1, blocks
    width = keep.shape[1]
    while left > 4:
        total = keep + exchange(send, "mp", by).astype(jnp.float32)
        total = total.reshape(left // 4, 2, block, width)
        keep = total[:, 0].reshape(-1, width)
        send = total[:, 1].reshape(-1, width).astype(jnp.bfloat16)
        by, left = by * 2, left // 2
    return keep, exchange(send, "mp", by)


def body(activations, norm_gain, norm_shift, up_weight, up_bias):
    blocks = lax.axis_size("mp")
    tokens = activations.shape[1] * lax.axis_size("dp")
    block = tokens // blocks
    rows = (tokens + 16 + 127) // 128 * 128
    depth = up_weight.shape[1]
    tile, slots, first, steps = plan(up_weight.shape[2])

    pieces = gather(activations[0])
    direct = len(pieces) > 1
    ring = fetch(up_weight, tile, slots, first, rows)
    if not direct:
        pieces = [pieces[0][b * block : (b + 1) * block] for b in range(blocks)]

    _, high = steps[0]
    count = len(pieces)
    config = (count, direct, tile, slots, first, high, blocks, tokens)
    ring, x, stat = pl.pallas_call(
        functools.partial(open_kernel, config),
        out_shape=(
            pltpu.VMEM(ring.shape, ring.dtype),
            pltpu.VMEM((rows, depth), jnp.bfloat16),
            pltpu.VMEM((tokens, LANES), jnp.float32),
        ),
        in_specs=[VM] * (3 + count) + [HB],
        out_specs=(VM,) * 3,
        scratch_shapes=[pltpu.SemaphoreType.DMA((2 * PARTS,))],
        input_output_aliases={2 + count: 0},
        compiler_params=params(rows),
        cost_estimate=cost(10 * tokens * depth, depth * (high - first) * tile * 2),
        name="open",
    )(norm_gain, norm_shift, *pieces, ring, up_weight)
    stats = [stat] + [exchange(stat, "mp", j) for j in range(1, blocks)]

    low = high
    done, high = steps[1]
    ring, earlier = pl.pallas_call(
        functools.partial(raw_kernel, (tile, slots, low, high)),
        out_shape=(
            pltpu.VMEM(ring.shape, ring.dtype),
            pltpu.VMEM((tokens + KEPT, done * tile), jnp.float32),
        ),
        in_specs=[VM, VM, HB],
        out_specs=(VM,) * 2,
        scratch_shapes=[pltpu.SemaphoreType.DMA((2 * PARTS,))],
        input_output_aliases={1: 0},
        compiler_params=params(rows),
        cost_estimate=cost(2 * rows * depth * done * tile, depth * max(high - low, 1) * tile * 2),
        name="raw",
    )(x, ring, up_weight)

    groups = []
    waiting = []
    edges = []
    ready = None
    start = 0

    def join(ring):
        ring, kept, away = merge(*waiting.pop(0), ring, tile, rows)
        groups.append((kept, exchange(away, "mp", blocks // 2)))
        return ring

    last = len(steps) - 3
    for i, step in enumerate(steps[2:]):
        if len(waiting) > 1:
            ring = join(ring)
        ended = (edges[0], up_bias) + groups[0] if i == last and i > 2 else None
        ring, got = layer(
            x, ring, up_weight, tile, slots, done, step, stats, earlier, ended, blocks, tokens, high
        )
        if ended is not None:
            ready = got[2]
        waiting.append(halved(got[0], got[1], blocks, block))
        edges.append(start)
        start += got[0].shape[1]
        earlier = None
        done, high = step
    while waiting:
        join(None)
    if ready is not None:
        groups, edges = groups[1:], edges[1:]
    return finale(up_bias, ready, edges, groups, tile, rows)


def solution(mesh):
    in_specs = (
        P("section", "dp", "mp"),
        P("section", "mp"),
        P("section", "mp"),
        P("section", "mp", "dp"),
        P("section", "dp"),
    )
    out_specs = P("section", "mp", "dp")
    return jax.shard_map(body, mesh=mesh, in_specs=in_specs, out_specs=out_specs, check_vma=False)
```

```python
import functools

import jax
import jax.numpy as jnp
from jax import lax
from jax.experimental import pallas as pl
from jax.experimental.pallas import tpu as pltpu
from jax.sharding import PartitionSpec as P

EPS = 1e-05
LANES = 128
MIB = 1 << 20
VM = pl.BlockSpec(memory_space=pltpu.VMEM)
HB = pl.BlockSpec(memory_space=pl.ANY)
EXTRA = 16
PARTS = 2
PIECE = 2
TILES = 24
SLOTS = 13
FIRST = 8
STEPS = ((8, 13), (20, 20), (24, 24))


def plan(columns):
    if columns % (TILES * LANES) == 0 and columns >= TILES * 512:
        return columns // TILES, SLOTS, FIRST, STEPS
    tile = next(u for u in (256, 128, columns) if columns % u == 0)
    tiles = columns // tile
    return tile, tiles, tiles, ((tiles - tiles // 2, tiles), (tiles, tiles))


def params(rows):
    return pltpu.CompilerParams(vmem_limit_bytes=(24 if rows > 256 else 8) * MIB)


def cost(flops, read):
    return pl.CostEstimate(flops=int(flops), bytes_accessed=int(read), transcendentals=0)


def pieces_of(slots, low, high, size=PIECE):
    result = []
    while low < high:
        count = min(high - low, slots - low % slots, size)
        result.append((low, low + count))
        low += count
    return result


def fetches(weight, ring, sem, tile, slots, pieces):
    step = weight.shape[1] // PARTS
    result = []
    for n, (low, high) in enumerate(pieces):
        columns = (high - low) * tile
        copies = []
        for i in range(PARTS):
            rows = pl.ds(i * step, step)
            copies.append(
                pltpu.make_async_copy(
                    weight.at[0, rows, pl.ds(low * tile, columns)],
                    ring.at[rows, pl.ds(low % slots * tile, columns)],
                    sem.at[n * PARTS + i],
                )
            )
            copies[-1].start()
        result.append(copies)
    return result


def wait(copies):
    for copy in copies:
        copy.wait()


def semaphores(pieces):
    return [pltpu.SemaphoreType.DMA((max(1, len(pieces)) * PARTS,))]


def fetch_kernel(tile, slots, pieces, weight, ring, sem):
    for copies in fetches(weight, ring, sem, tile, slots, pieces):
        wait(copies)


def fetch(weight, tile, slots, first, rows):
    depth = weight.shape[1]
    pieces = pieces_of(slots, 0, first, first)
    return pl.pallas_call(
        functools.partial(fetch_kernel, tile, slots, pieces),
        out_shape=pltpu.VMEM((depth, slots * tile), weight.dtype),
        in_specs=[HB],
        out_specs=VM,
        scratch_shapes=semaphores(pieces),
        compiler_params=params(rows),
        cost_estimate=cost(0, depth * first * tile * 2),
        name="fetch",
    )(weight)


def packed(average, spread):
    lane = lax.broadcasted_iota(jnp.int32, (average.shape[0], LANES), 1)
    return jnp.where(lane < LANES // 2, average, spread)


def unpacked(stat):
    return stat[:, 0:1], stat[:, LANES // 2 : LANES // 2 + 1]


def encoded(average, spread):
    lane = lax.broadcasted_iota(jnp.int32, (average.shape[0], LANES), 1)
    result = jnp.zeros(lane.shape, jnp.float32)
    for base, value in ((0, average), (3, spread)):
        for i in range(3):
            piece = value.astype(jnp.bfloat16).astype(jnp.float32)
            result = jnp.where(lane == base + i, piece, result)
            value = value - piece
    return result.astype(jnp.bfloat16)


def decoded(code):
    values = code.astype(jnp.float32)
    return (
        values[:, 0:1] + values[:, 1:2] + values[:, 2:3],
        values[:, 3:4] + values[:, 4:5] + values[:, 5:6],
    )


def prepare(places, gain, shift, pieces, x_ref, stat_ref):
    rows, width = pieces[0].shape
    tokens = rows * len(pieces)
    gains = gain[...].astype(jnp.float32)
    shifts = shift[...].astype(jnp.float32)
    for k, piece in enumerate(pieces):
        for sub in range(rows // 16):
            values = piece[pl.ds(sub * 16, 16), :].astype(jnp.float32)
            average = jnp.sum(values, axis=1, keepdims=True) / width
            centred = values - average
            spread = jnp.sum(centred * centred, axis=1, keepdims=True)
            place = pl.ds(pl.multiple_of(places[k] + sub * 16, 16), 16)
            x_ref[place, :] = (centred * gains).astype(jnp.bfloat16)
            stat_ref[place, :] = packed(average, spread)
    row = lax.broadcasted_iota(jnp.int32, (EXTRA, width), 0)
    x_ref[pl.ds(tokens, EXTRA), :] = jnp.where(row % 2 == 0, gains, shifts).astype(jnp.bfloat16)
    rest = x_ref.shape[0] - tokens - EXTRA
    x_ref[pl.ds(tokens + EXTRA, rest), :] = jnp.zeros((rest, width), jnp.bfloat16)


def product(x_ref, ring, tile, slots, index):
    at = pl.ds(pl.multiple_of(lax.rem(index, slots) * tile, tile), tile)
    return jnp.dot(x_ref[...], ring[:, at], preferred_element_type=jnp.float32)


def extras(rows):
    high = rows.astype(jnp.bfloat16).astype(jnp.float32)
    return jnp.concatenate([high, rows - high], axis=0).astype(jnp.bfloat16)


def sum_of(code):
    values = code.astype(jnp.float32)
    return values[:8] + values[8:]


def chunk(config, x_ref, ring, stat_ref, outs, coming, fetched):
    blocks, tile, slots, base, done, low, tokens, origin = config
    send, keep, rows, kept_stat = outs
    block = tokens // blocks
    half = tokens // 2
    width = keep.shape[1]

    def multiply(first, last):
        @pl.loop(first, last)
        def _(i):
            acc = product(x_ref, ring, tile, slots, i)
            at = pl.ds(pl.multiple_of((i - origin) * tile, tile), tile)
            for j in range(blocks):
                place = send if j % 2 else keep
                part = acc[j * block : (j + 1) * block]
                place[pl.ds((j // 2) * block, block), at] = part.astype(place.dtype)
            rows[:, at] = acc[tokens : tokens + 8]
            send[pl.ds(half, EXTRA), at] = extras(acc[tokens : tokens + 8])

    multiply(base, min(low, done))
    last = pl.ds(width, LANES)
    for j in range(blocks) if base == origin else ():
        stat = stat_ref[pl.ds(j * block, block), :]
        place = pl.ds((j // 2) * block, block)
        if j % 2:
            send[place, last] = encoded(*unpacked(stat))
        else:
            kept_stat[place, :] = stat
    if base == origin:
        send[pl.ds(half, EXTRA), last] = jnp.zeros((EXTRA, LANES), send.dtype)
    for (first, end), copies in zip(fetched, coming):
        wait(copies)
        if first < done:
            multiply(first, min(end, done))


def open_kernel(config, count, direct, fetched, *refs):
    blocks, total = config[0], config[6]
    tile, slots = config[1:3]
    gain, shift = refs[:2]
    pieces = refs[2 : 2 + count]
    _, weight, ring, x_ref, stat_ref, *outs, sem = refs[2 + count :]
    coming = fetches(weight, ring, sem, tile, slots, fetched)

    mine = lax.axis_index("mp")
    size = pieces[0].shape[0]
    block = total // blocks
    owners = list(range(blocks))
    if direct:
        me = lax.axis_index("dp")
        owners = [lax.rem(me + count - k, count) for k in range(count)]
    places = [((o * size // block) ^ mine) * block + (o * size) % block for o in owners]

    @pl.when(mine >= 0)
    def _():
        prepare(places, gain, shift, pieces, x_ref, stat_ref)

    chunk(config, x_ref, ring, stat_ref, outs, coming, fetched)


def layer_kernel(config, fetched, earlier, x_ref, _, weight, stat_ref, *refs):
    ring = refs[earlier]
    coming = fetches(weight, ring, refs[-1], config[1], config[2], fetched)
    chunk(config, x_ref, ring, stat_ref, refs[-5:-1], coming, fetched)


def outputs(tokens, width):
    half = tokens // 2
    return (
        pltpu.VMEM((half + EXTRA, width + LANES), jnp.bfloat16),
        pltpu.VMEM((half, width), jnp.float32),
        pltpu.VMEM((8, width), jnp.float32),
        pltpu.VMEM((half, LANES), jnp.float32),
    )


def layer(x, ring, weight, stat, config, high, earlier, end):
    blocks, tile, slots, base, done, low, tokens, origin = config
    rows = x.shape[0]
    depth = weight.shape[1]
    fetched = pieces_of(slots, low, high, 1 if done == high else PIECE)
    read = depth * max(high - low, (done - base) / 2) * tile * 2
    return pl.pallas_call(
        functools.partial(layer_kernel, config, fetched, len(earlier)),
        out_shape=(pltpu.VMEM(ring.shape, ring.dtype),) + outputs(tokens, (end - origin) * tile),
        in_specs=[VM, VM, HB, VM] + [VM] * len(earlier),
        out_specs=(VM,) * 5,
        scratch_shapes=semaphores(fetched),
        input_output_aliases={1: 0} | {4 + n: 1 + n for n in range(len(earlier))},
        compiler_params=params(rows),
        cost_estimate=cost(2 * rows * depth * (done - base) * tile, read),
        name="layer",
    )(x, ring, weight, stat, *earlier)


def compact(width):
    return width % (8 * LANES) == 0


def across(column, width):
    high = column.shape[0]
    return jnp.concatenate([jnp.broadcast_to(column, (high, LANES))] * (width // LANES), axis=1)


def stride(widths, tile):
    return next(n * tile for n in (2, 1) if all(width % (n * tile) == 0 for width in widths))


def merge_kernel(config, count, *refs):
    tile, block, features, final = config
    parts = [refs[3 * n : 3 * n + 3] for n in range(count)]
    stat = refs[3 * count]
    kept, rows_out, stat_out, away = refs[-4:]
    high, width = parts[0][0].shape[0], kept.shape[1]
    blocks = high // block
    average, spread = unpacked(stat[...])
    first = parts[0][2]
    other, other_spread = decoded(first[pl.ds(0, high), pl.ds(first.shape[1] - LANES, LANES)])
    apart = average - other
    average = (average + other) / 2
    spread = spread + other_spread + apart * apart * (features / 2)
    folded = final and compact(width)
    tile = stride([keep.shape[1] for keep, _, _ in parts], tile)
    aside = across(apart / 2, tile)

    start = 0
    for keep, rows, got in parts:

        @pl.loop(0, keep.shape[1] // tile)
        def _(i, keep=keep, rows=rows, got=got, start=start):
            at = pl.ds(pl.multiple_of(i * tile, tile), tile)
            to = pl.ds(pl.multiple_of(start + i * tile, tile), tile)
            mine = rows[:, at]
            others = sum_of(got[pl.ds(high, EXTRA), at])
            total = keep[:, at] + got[pl.ds(0, high), at].astype(jnp.float32)
            total = total + aside * (mine[0:1] - others[0:1])
            for k in range(blocks):
                place = away if k % 2 else kept
                part = total[k * block : (k + 1) * block]
                place[pl.ds((k // 2) * block, block), to] = part.astype(place.dtype)
            rows_out[:, to] = mine + others
            if not folded:
                away[pl.ds(high // 2, EXTRA), to] = extras(mine + others)

        start += keep.shape[1]

    last = pl.ds(away.shape[1] - LANES, LANES)
    for k in range(blocks):
        part = slice(k * block, (k + 1) * block)
        place = pl.ds((k // 2) * block, block)
        if k % 2:
            away[place, last] = encoded(average[part], spread[part])
        else:
            stat_out[place, :] = packed(average[part], spread[part])
    if folded:
        fold = width // 8
        lines = [rows_out[r : r + 1, i * fold : (i + 1) * fold] for r in (0, 1) for i in range(8)]
        away[:, pl.ds(width, fold)] = jnp.concatenate(lines, axis=0).astype(away.dtype)
    else:
        away[pl.ds(high // 2, EXTRA), last] = jnp.zeros((EXTRA, LANES), away.dtype)


def merge(parts, stat, ring, tied, config, total):
    tile, block, features, final = config
    half = parts[0][0].shape[0] // 2
    width = sum(keep.shape[1] for keep, _, _ in parts)
    args = [one for part in parts for one in part] + [stat]
    through = [] if ring is None else [ring]
    outs = [pltpu.VMEM(ring.shape, ring.dtype)] if through else []
    outs.append(pltpu.VMEM((half, width), jnp.float32))
    outs.append(pltpu.VMEM((8, width), jnp.float32))
    outs.append(pltpu.VMEM((half, LANES), jnp.float32))
    if final and compact(width):
        outs.append(pltpu.VMEM((half, width + width // 8 + LANES), jnp.bfloat16))
    else:
        outs.append(pltpu.VMEM((half + EXTRA, width + LANES), jnp.bfloat16))
    result = pl.pallas_call(
        functools.partial(merge_kernel, config, len(parts)),
        out_shape=tuple(outs),
        in_specs=[VM] * (len(args) + len(through)) + [HB] * len(tied),
        out_specs=(VM,) * len(outs),
        input_output_aliases={len(args): 0} if through else {},
        compiler_params=params(total),
        name="merge",
    )(*args, *through, *tied)
    ring, result = (result[0], result[1:]) if through else (None, result)
    return ring, result[:3], result[3]


def finish_kernel(config, bias, kept, rows, stat, got, *refs):
    low, tile, features = config
    whole, part, unfolded, sem = refs[-4:]
    height, width = kept.shape
    average, spread = unpacked(stat[...])
    other, other_spread = decoded(got[pl.ds(0, height), pl.ds(got.shape[1] - LANES, LANES)])
    apart = average - other
    spread = spread + other_spread + apart * apart * (features / 2)
    scale = lax.rsqrt(spread / (2 * features) + EPS)
    folded = compact(width)
    tile = stride([width], tile)
    aside = across(apart / 2, tile)
    scale = across(scale, tile)
    if folded:
        fold = width // 8
        code = got[:, pl.ds(width, fold)].astype(jnp.float32)
        for i in range(8):
            unfolded[0:1, i * fold : (i + 1) * fold] = code[i : i + 1]
            unfolded[1:2, i * fold : (i + 1) * fold] = code[8 + i : 9 + i]

    @pl.loop(0, width // tile)
    def _(i):
        at = pl.multiple_of(i * tile, tile)
        here = pl.ds(at, tile)
        mine = rows[:, here]
        others = unfolded[:, here] if folded else sum_of(got[pl.ds(height, EXTRA), here])
        total = kept[:, here] + got[pl.ds(0, height), here].astype(jnp.float32)
        total = total + aside * (mine[0:1] - others[0:1])
        total = scale * total + (mine[1:2] + others[1:2])
        total = total + bias[:, pl.ds(pl.multiple_of(low + at, tile), tile)].astype(jnp.float32)
        part[:, here] = jax.nn.gelu(total, approximate=True).astype(part.dtype)

    copy = pltpu.make_async_copy(part, whole.at[0, :, pl.ds(low, width)], sem)
    copy.start()
    copy.wait()


def finish(bias, low, mine, got, whole, tile, features, total):
    args = [bias, *mine, got] + ([] if whole is None else [whole])
    height, width = mine[0].shape
    return pl.pallas_call(
        functools.partial(finish_kernel, (low, tile, features)),
        out_shape=jax.ShapeDtypeStruct((1, height, bias.shape[1]), jnp.bfloat16),
        in_specs=[VM] * 5 + [HB] * (len(args) - 5),
        out_specs=HB,
        scratch_shapes=[
            pltpu.VMEM((height, width), jnp.bfloat16),
            pltpu.VMEM((8, width), jnp.float32),
            pltpu.SemaphoreType.DMA,
        ],
        input_output_aliases={} if whole is None else {5: 0},
        compiler_params=params(total),
        cost_estimate=cost(20 * height * width, height * width * 8),
        name="finish",
    )(*args)


def exchange(value, axis, by):
    size = lax.axis_size(axis)
    return lax.ppermute(value, axis, [(i, i ^ by) for i in range(size)])


def gather(block):
    sections, places = lax.axis_size("section"), lax.axis_size("dp")
    if places > 8:
        received = lax.ppermute(
            block, "section", [(s, (s + 1) % sections) for s in range(sections)]
        )
        return [lax.all_gather(received, "dp", axis=0, tiled=True)]
    pieces = []
    for k in range(places):
        pairs = [
            (s * places + d, ((s + 1) % sections) * places + (d + k) % places)
            for s in range(sections)
            for d in range(places)
        ]
        pieces.append(lax.ppermute(block, ("section", "dp"), pairs))
    return pieces


def body(activations, norm_gain, norm_shift, up_weight, up_bias):
    blocks = lax.axis_size("mp")
    tokens = activations.shape[1] * lax.axis_size("dp")
    block = tokens // blocks
    rows = (tokens + EXTRA + 127) // 128 * 128
    depth = up_weight.shape[1]
    tile, slots, first, steps = plan(up_weight.shape[2])

    pieces = gather(activations[0])
    direct = len(pieces) > 1
    ring = fetch(up_weight, tile, slots, first, rows)
    if not direct:
        pieces = [pieces[0][b * block : (b + 1) * block] for b in range(blocks)]

    count = len(pieces)
    done, high = steps[0]
    fetched = pieces_of(slots, first, high)
    joint = steps[-2][0] if len(steps) > 2 else done
    config = (blocks, tile, slots, 0, done, first, tokens, 0)
    ring, x, stat, *made = pl.pallas_call(
        functools.partial(open_kernel, config, count, direct, fetched),
        out_shape=(
            pltpu.VMEM(ring.shape, ring.dtype),
            pltpu.VMEM((rows, depth), jnp.bfloat16),
            pltpu.VMEM((tokens, LANES), jnp.float32),
        )
        + outputs(tokens, joint * tile),
        in_specs=[VM] * (3 + count) + [HB],
        out_specs=(VM,) * 7,
        scratch_shapes=semaphores(fetched),
        input_output_aliases={2 + count: 0},
        compiler_params=params(rows),
        cost_estimate=cost(2 * rows * depth * done * tile, depth * max(high - first, 1) * tile * 2),
        name="open",
    )(norm_gain, norm_shift, *pieces, ring, up_weight)

    groups = []
    waiting = []

    def post(made):
        waiting.append((made[1:], exchange(made[0], "mp", 1)))

    def join(ring, start):
        tied = []
        stat = waiting[0][0][2]
        parts = [(keep, lines, got) for (keep, lines, _), got in waiting]
        waiting.clear()
        by = 1
        while 2 * by < blocks:
            config = (tile, block, depth * by, 4 * by == blocks)
            ring, part, away = merge(parts, stat, ring, tied, config, rows)
            by *= 2
            got = exchange(away, "mp", by)
            parts, stat = [(part[0], part[1], got)], part[2]
        groups.append((start, part, got))
        return ring

    for step in steps[1:-1]:
        config = (blocks, tile, slots, done, step[0], high, tokens, 0)
        ring, *made = layer(x, ring, up_weight, stat, config, step[1], made, joint)
        done, high = step
    post(made)
    ring = join(ring, 0)
    config = (blocks, tile, slots, done, steps[-1][0], high, tokens, done)
    ring, *made = layer(x, ring, up_weight, stat, config, steps[-1][1], [], steps[-1][0])
    post(made)
    join(None, done * tile)
    whole = None
    for low, part, got in groups:
        whole = finish(up_bias, low, part, got, whole, tile, depth * blocks // 2, rows)
    return whole


def solution(mesh):
    in_specs = (
        P("section", "dp", "mp"),
        P("section", "mp"),
        P("section", "mp"),
        P("section", "mp", "dp"),
        P("section", "dp"),
    )
    out_specs = P("section", "mp", "dp")
    return jax.shard_map(body, mesh=mesh, in_specs=in_specs, out_specs=out_specs, check_vma=False)
```
